32 devices in a mesh: dp: 4 (over z), row: 2 (over core), col: 4 (over y, x).
Axes of the slice: x: 2, y: 2, z: 4, core: 2. Of those that a mesh axis runs over, the one named last changes fastest.
Arguments:
- features: bfloat16 [2048, 4096], P(('dp', 'row')), may hold values from -6 to 6
- w_in: bfloat16 [4096, 4096], P('row', 'col'), may hold values from -0.09375 to 0.09375
- w_out: bfloat16 [4096, 1024], P('col'), may hold values from -0.09375 to 0.09375
- captions: bfloat16 [2048, 1024], P(('dp', 'row', 'col')), may hold values from -6 to 6
- positive: int32 [2048], P(('dp', 'row')), may hold values from 0 to 2047, each once
Outputs:
- fig_terms: float32 [2048], P(('dp', 'row'))
- cap_terms: float32 [2048], P(('dp', 'row', 'col'))
- grad_w_in: float32 [4096, 4096], P(('dp', 'row'), 'col')
- grad_w_out: float32 [4096, 1024], P('col', ('dp', 'row'))
The draws below stay inside these ranges and needn't reach their ends.
Inputs may be any that keep to these rules, and one draw needn't show every extreme that they name: positive is a permutation: every caption is the match of exactly one figure.
All inputs are finite; a program needn't handle non-finite values.
Results may differ from the reference program's by a relative error of at most 0.0053.
Values may be sent and summed in bfloat16 or wider, within the bound.
A program may use at most 128 MiB of HBM per device.

```python
import jax
import jax.numpy as jnp
from jax import lax

DIN = 4096
HID = 4096
EMB = 1024
BATCH = 2048


def shard_levels(key, shape, split, smallest, top_value):
    factor_of = 1.0
    for position, shards_of in split:
        heights = jax.random.uniform(jax.random.fold_in(jax.random.fold_in(key, 6), position), (shards_of,), jnp.float32, smallest / len(split), top_value / len(split))
        factor_of = factor_of * jnp.repeat(jnp.exp(heights), shape[position] // shards_of).reshape((-1,) + (1,) * (len(shape) - 1 - position))
    return factor_of


def bell_draw(stream_key, extent, spread, most, cuts=(), kind=jnp.bfloat16):
    result = jax.random.normal(stream_key, extent, jnp.float32) * spread
    if len(cuts) > 0:
        result = shard_levels(stream_key, extent, cuts, -0.22, 0.18) * result
    return jnp.clip(result, min=-most, max=most).astype(kind)


def setup_inputs(seed: int = 0) -> dict:
    streams_of = jax.random.split(jax.random.key(seed), 6)
    features = bell_draw(streams_of[0], (BATCH, DIN), 1.0, 6.0, ((0, 8),))
    w_in = bell_draw(streams_of[1], (DIN, HID), DIN ** -0.5, 0.09375, ((0, 2), (1, 4)))
    w_out = bell_draw(streams_of[2], (HID, EMB), HID ** -0.5, 0.09375, ((0, 4),))
    captions = bell_draw(streams_of[3], (BATCH, EMB), 1.0, 6.0, ((0, 32),))
    positive = jax.random.permutation(streams_of[4], BATCH).astype(jnp.int32)
    return {"features": features, "w_in": w_in, "w_out": w_out, "captions": captions, "positive": positive}


SCALE = 50.0
EPS = 1e-06

def gelu_back(pre, grad):
    return jax.vjp(jax.nn.gelu, pre)[1](grad)[0]

def reference(features, w_in, w_out, captions, positive):
    pre = jnp.dot(features, w_in, preferred_element_type=jnp.float32)
    hidden = jax.nn.gelu(pre).astype(jnp.bfloat16)
    emb = jnp.dot(hidden, w_out, preferred_element_type=jnp.float32)
    inv = lax.rsqrt(lax.optimization_barrier(jnp.sum(emb * emb, axis=1, keepdims=True)) + EPS)
    fhat = emb * inv
    fhat_b = fhat.astype(jnp.bfloat16)
    cap32 = captions.astype(jnp.float32)
    chat = (cap32 * lax.rsqrt(lax.optimization_barrier(jnp.sum(cap32 * cap32, axis=1, keepdims=True)) + EPS)).astype(jnp.bfloat16)
    total = fhat_b.shape[0]
    blk = min(512, total)
    nblk = total // blk
    fb_blocks = fhat_b.reshape(nblk, blk, -1)
    pos_blocks = positive.reshape(nblk, blk)
    colids = jnp.arange(total, dtype=jnp.int32)

    def block_logits(fb, pos):
        logits = SCALE * jnp.dot(fb, chat.T, preferred_element_type=jnp.float32)
        mask = (pos[:, None] == colids[None, :]).astype(jnp.float32)
        return (logits, mask)

    def first_pass(carry, inputs):
        fb, pos = inputs
        logits, mask = block_logits(fb, pos)
        expo = jnp.exp(logits)
        picked = mask * logits
        return ((carry[0] + lax.optimization_barrier(jnp.sum(expo, axis=0)), carry[1] + lax.optimization_barrier(jnp.sum(picked, axis=0))), (lax.optimization_barrier(jnp.sum(expo, axis=1)), lax.optimization_barrier(jnp.sum(picked, axis=1))))
    zeros = jnp.zeros((total,), jnp.float32)
    (colsum, colpos), (rowsum, rowpos) = lax.scan(first_pass, (zeros, zeros), (fb_blocks, pos_blocks))
    rowsum = rowsum.reshape(total)
    rowpos = rowpos.reshape(total)
    fig_terms = jnp.log(rowsum) - rowpos
    cap_terms = jnp.log(colsum) - colpos

    def second_pass(carry, inputs):
        fb, pos, rsum = inputs
        logits, mask = block_logits(fb, pos)
        expo = jnp.exp(logits)
        dlog = (expo / rsum[:, None] + expo / colsum[None, :] - 2.0 * mask).astype(jnp.bfloat16)
        return (carry, SCALE * jnp.dot(dlog, chat, preferred_element_type=jnp.float32))
    _, dfhat = lax.scan(second_pass, 0.0, (fb_blocks, pos_blocks, rowsum.reshape(nblk, blk)))
    dfhat = dfhat.reshape(total, -1)
    demb = ((dfhat - fhat * lax.optimization_barrier(jnp.sum(fhat * dfhat, axis=1, keepdims=True))) * inv).astype(jnp.bfloat16)
    dh = jnp.dot(demb, w_out.T, preferred_element_type=jnp.float32)
    dpre = gelu_back(pre, dh).astype(jnp.bfloat16)
    grad_w_out = jnp.dot(hidden.T, demb, preferred_element_type=jnp.float32)
    grad_w_in = jnp.dot(features.T, dpre, preferred_element_type=jnp.float32)
    return (fig_terms, cap_terms, grad_w_in, grad_w_out)
```

```python
import jax
import jax.numpy as jnp
from jax import lax
from jax.sharding import PartitionSpec as P

SCALE = 50.0
EPS = 1e-06


def gelu_back(pre, grad):
    return jax.vjp(jax.nn.gelu, pre)[1](grad)[0]


def on_device(features, w_in, w_out, captions, positive):
    group = ("dp", "row")
    every = ("dp", "row", "col")
    f32 = jnp.float32
    slices = lax.all_to_all(features, group, 1, 0, tiled=True)
    cap32 = captions.astype(f32)
    chat_local = (cap32 * lax.rsqrt(jnp.sum(cap32 * cap32, axis=1, keepdims=True) + EPS)).astype(
        jnp.bfloat16
    )
    chat = lax.all_gather(chat_local, every, axis=0, tiled=True)
    pre = jnp.dot(
        features, lax.all_gather(w_in, "row", axis=0, tiled=True), preferred_element_type=f32
    )
    hidden = jax.nn.gelu(pre).astype(jnp.bfloat16)
    part = jnp.dot(hidden, w_out, preferred_element_type=f32)
    emb = lax.psum_scatter(part, "col", scatter_dimension=0, tiled=True)
    mine = emb.shape[0]
    inv = lax.rsqrt(jnp.sum(emb * emb, axis=1, keepdims=True) + EPS)
    fhat = emb * inv
    fhat_b = fhat.astype(jnp.bfloat16)
    logits = SCALE * lax.dot_general(
        fhat_b, chat, (((1,), (1,)), ((), ())), preferred_element_type=f32
    )
    col = lax.axis_index("col")
    places = lax.dynamic_slice_in_dim(positive, col * mine, mine, 0)
    colids = jnp.arange(chat.shape[0], dtype=jnp.int32)
    mask = (places[:, None] == colids[None, :]).astype(f32)
    expo = jnp.exp(logits)
    picked = mask * logits
    rowsum, rowpos = jnp.sum(expo, axis=1), jnp.sum(picked, axis=1)
    colsum, colpos = lax.psum((jnp.sum(expo, axis=0), jnp.sum(picked, axis=0)), every)
    fig_terms = lax.all_gather(jnp.log(rowsum) - rowpos, "col", axis=0, tiled=True)
    capdev = captions.shape[0]
    place = (lax.axis_index("dp") * lax.axis_size("row") + lax.axis_index("row")) * lax.axis_size(
        "col"
    ) + col
    cap_terms = lax.dynamic_slice_in_dim(jnp.log(colsum) - colpos, place * capdev, capdev, 0)
    dlog = (expo / rowsum[:, None] + expo / colsum[None, :] - 2.0 * mask).astype(jnp.bfloat16)
    dfhat = SCALE * jnp.dot(dlog, chat, preferred_element_type=f32)
    demb = ((dfhat - fhat * jnp.sum(fhat * dfhat, axis=1, keepdims=True)) * inv).astype(
        jnp.bfloat16
    )
    demb = lax.all_gather(demb, "col", axis=0, tiled=True)
    dh = lax.dot_general(demb, w_out, (((1,), (1,)), ((), ())), preferred_element_type=f32)
    dpre = gelu_back(pre, dh).astype(jnp.bfloat16)
    dpre_all = lax.all_gather(dpre, group, axis=0, tiled=True)
    head_term = lax.dot_general(
        hidden, demb, (((0,), (0,)), ((), ())), preferred_element_type=f32
    )
    grad_w_out = lax.psum_scatter(head_term, group, scatter_dimension=1, tiled=True)
    grad_w_in = lax.dot_general(
        slices, dpre_all, (((0,), (0,)), ((), ())), preferred_element_type=f32
    )
    return (fig_terms, cap_terms, grad_w_in, grad_w_out)


def solution(mesh):
    placed = (
        P(("dp", "row"), None),
        P("row", "col"),
        P("col", None),
        P(("dp", "row", "col"), None),
        P(("dp", "row")),
    )
    return jax.shard_map(
        on_device,
        mesh=mesh,
        in_specs=placed,
        out_specs=(
            P(("dp", "row")),
            P(("dp", "row", "col")),
            P(("dp", "row"), "col"),
            P("col", ("dp", "row")),
        ),
        check_vma=False,
    )
```

```python
import functools

import jax
import jax.numpy as jnp
from jax import lax
from jax.experimental import pallas as pl
from jax.experimental.pallas import tpu as pltpu
from jax.sharding import PartitionSpec as P

SCALE = 50.0
EPS = 1e-06


def gelu_back(pre, grad):
    return jax.vjp(jax.nn.gelu, pre)[1](grad)[0]


def plain(features, w_in, w_out, captions, positive):
    group = ("dp", "row")
    every = ("dp", "row", "col")
    f32 = jnp.float32
    slices = lax.all_to_all(features, group, 1, 0, tiled=True)
    cap32 = captions.astype(f32)
    chat_local = (cap32 * lax.rsqrt(jnp.sum(cap32 * cap32, axis=1, keepdims=True) + EPS)).astype(
        jnp.bfloat16
    )
    chat = lax.all_gather(chat_local, every, axis=0, tiled=True)
    pre = jnp.dot(
        features, lax.all_gather(w_in, "row", axis=0, tiled=True), preferred_element_type=f32
    )
    hidden = jax.nn.gelu(pre).astype(jnp.bfloat16)
    part = jnp.dot(hidden, w_out, preferred_element_type=f32)
    emb = lax.psum_scatter(part, "col", scatter_dimension=0, tiled=True)
    mine = emb.shape[0]
    inv = lax.rsqrt(jnp.sum(emb * emb, axis=1, keepdims=True) + EPS)
    fhat = emb * inv
    fhat_b = fhat.astype(jnp.bfloat16)
    logits = SCALE * lax.dot_general(
        fhat_b, chat, (((1,), (1,)), ((), ())), preferred_element_type=f32
    )
    col = lax.axis_index("col")
    places = lax.dynamic_slice_in_dim(positive, col * mine, mine, 0)
    colids = jnp.arange(chat.shape[0], dtype=jnp.int32)
    mask = (places[:, None] == colids[None, :]).astype(f32)
    expo = jnp.exp(logits)
    picked = mask * logits
    rowsum, rowpos = jnp.sum(expo, axis=1), jnp.sum(picked, axis=1)
    colsum, colpos = lax.psum((jnp.sum(expo, axis=0), jnp.sum(picked, axis=0)), every)
    fig_terms = lax.all_gather(jnp.log(rowsum) - rowpos, "col", axis=0, tiled=True)
    capdev = captions.shape[0]
    place = (lax.axis_index("dp") * lax.axis_size("row") + lax.axis_index("row")) * lax.axis_size(
        "col"
    ) + col
    cap_terms = lax.dynamic_slice_in_dim(jnp.log(colsum) - colpos, place * capdev, capdev, 0)
    dlog = (expo / rowsum[:, None] + expo / colsum[None, :] - 2.0 * mask).astype(jnp.bfloat16)
    dfhat = SCALE * jnp.dot(dlog, chat, preferred_element_type=f32)
    demb = ((dfhat - fhat * jnp.sum(fhat * dfhat, axis=1, keepdims=True)) * inv).astype(
        jnp.bfloat16
    )
    demb = lax.all_gather(demb, "col", axis=0, tiled=True)
    dh = lax.dot_general(demb, w_out, (((1,), (1,)), ((), ())), preferred_element_type=f32)
    dpre = gelu_back(pre, dh).astype(jnp.bfloat16)
    dpre_all = lax.all_gather(dpre, group, axis=0, tiled=True)
    head_term = lax.dot_general(
        hidden, demb, (((0,), (0,)), ((), ())), preferred_element_type=f32
    )
    grad_w_out = lax.psum_scatter(head_term, group, scatter_dimension=1, tiled=True)
    grad_w_in = lax.dot_general(
        slices, dpre_all, (((0,), (0,)), ((), ())), preferred_element_type=f32
    )
    return (fig_terms, cap_terms, grad_w_in, grad_w_out)


MESH = pl.DeviceIdType.MESH
ROOT = 0.7978845608028654
CUBE = 0.044715
TILE = 256


def gelu_and_slope(x):
    t = jnp.tanh(ROOT * (x + CUBE * x * x * x))
    half = 0.5 * (1.0 + t)
    return x * half, half + 0.5 * x * (1.0 - t * t) * (ROOT * (1.0 + 3.0 * CUBE * x * x))


def remote(src, dst, send, recv, where):
    return pltpu.make_async_remote_copy(
        src_ref=src, dst_ref=dst, send_sem=send, recv_sem=recv, device_id=where, device_id_type=MESH
    )


def dot(a, b, ca, cb):
    return lax.dot_general(a, b, (((ca,), (cb,)), ((), ())), preferred_element_type=jnp.float32)


def kernel(nd, nr, nc, feat, w_in, w_out, caps, pos, ids,
           fig_out, cap_out, gwi, gwo,
           fsib, psend, precv, pre, slope, hidden, part, esend, erecv, fhat, chat, expo, dlog,
           dfh, demb, dpre, slices, stage, stat, head, hsum, hsib, hup, hdn,
           s_f, r_f, s_p, r_p, s_c1, r_c1, s_c2, r_c2, s_c3, r_c3, s_e, r_e,
           s_x1, r_x1, s_x2, r_x2, s_x3, r_x3, s_d, r_d, s_t, r_t,
           s_a, r_a, s_b, r_b, s_g, r_g, s_up, r_up, s_dn, r_dn, s_sib, r_sib,
           s_h, r_h, s_hu, r_hu, s_hd, r_hd):
    f32, bf16 = jnp.float32, jnp.bfloat16
    d, r, c = lax.axis_index("dp"), lax.axis_index("row"), lax.axis_index("col")
    other = 1 - r
    sib = (d, other, c)
    rows = feat.shape[0]
    half = w_in.shape[0]
    hid = w_in.shape[1]
    emb = w_out.shape[1]
    mine = rows // nc
    cap = caps.shape[0]
    total = chat.shape[0]
    width = gwi.shape[0]
    lanes = gwo.shape[1]
    tiles = hid // TILE

    def col_of(j):
        return lax.rem(c + j, nc)

    def dp_of(j):
        return lax.rem(d + j, nd)

    def at(index, size):
        return pl.ds(pl.multiple_of(index * size, size), size)

    barrier = pltpu.get_barrier_semaphore()
    pl.semaphore_signal(barrier, inc=1, device_id=sib, device_id_type=MESH)
    for j in range(1, nc):
        pl.semaphore_signal(barrier, inc=1, device_id=(d, r, col_of(j)), device_id_type=MESH)
    for j in range(1, nd):
        pl.semaphore_signal(barrier, inc=1, device_id=(dp_of(j), r, c), device_id_type=MESH)
    pl.semaphore_wait(barrier, nc + nd - 1)
    sent = []

    def go(*a):
        cp = remote(*a)
        cp.start()
        sent.append(cp)
        return cp

    cf = go(feat.at[:, at(other, half)], fsib, s_f, r_f, sib)
    cap32 = caps[...].astype(f32)
    slot = (r * nc + c) * nd + d
    chat[at(slot, cap), :] = (
        cap32 * lax.rsqrt(jnp.sum(cap32 * cap32, axis=1, keepdims=True) + EPS)
    ).astype(bf16)
    c1 = [
        go(chat.at[at(slot, cap)], chat.at[at(slot, cap)], s_c1.at[j], r_c1.at[j], (dp_of(j), r, c))
        for j in range(1, nd)
    ]
    mark = at(d * nr + r, rows)
    ca, cb = [], []
    for j in range(1, nd):
        to = dp_of(j)
        ca.append(go(feat.at[:, at(to * nr + r, width)], slices.at[mark], s_a.at[j], r_a.at[j], (to, r, c)))
        cb.append(go(feat.at[:, at(to * nr + other, width)], stage.at[d], s_b.at[j], r_b.at[j], (to, r, c)))
    go(feat.at[:, at(d * nr + other, width)], slices.at[mark], s_g.at[0], r_g.at[0], sib)
    slices[mark, :] = feat[:, at(d * nr + r, width)]

    @pl.loop(0, tiles)
    def _(k):
        pre[:, at(k, TILE)] = dot(feat[:, at(r, half)], w_in[:, at(k, TILE)], 1, 0)

    cf.wait_recv()

    @pl.loop(0, tiles)
    def _(k):
        psend[k] = dot(fsib[...], w_in[:, at(k, TILE)], 1, 0)
        remote(psend.at[k], precv.at[k], s_p.at[k], r_p.at[k], sib).start()

    @pl.loop(0, tiles)
    def _(k):
        remote(psend.at[k], precv.at[k], s_p.at[k], r_p.at[k], sib).wait()
        x = pre[:, at(k, TILE)] + precv[k]
        h, g = gelu_and_slope(x)
        hidden[:, at(k, TILE)] = h.astype(bf16)
        slope[:, at(k, TILE)] = g

    for cp in c1:
        cp.wait_recv()
    c2 = []
    line = at(r * nc + c, nd * cap)
    for j in range(1, nc):
        c2.append(go(chat.at[line], chat.at[line], s_c2.at[j], r_c2.at[j], (d, r, col_of(j))))

    @pl.loop(0, emb // TILE)
    def _(k):
        part[:, at(k, TILE)] = dot(hidden[...], w_out[:, at(k, TILE)], 1, 0)

    ce = []
    for j in range(1, nc):
        esend[j] = part[at(col_of(j), mine), :].astype(bf16)
        ce.append(go(esend.at[j], erecv.at[j], s_e.at[j], r_e.at[j], (d, r, col_of(j))))
    e = part[at(c, mine), :]
    for j in range(1, nc):
        ce[j - 1].wait_recv()
        e = e + erecv[j].astype(f32)
    inv = lax.rsqrt(jnp.sum(e * e, axis=1, keepdims=True) + EPS)
    fhat[...] = e * inv
    for cp in c2:
        cp.wait_recv()
    c3 = go(chat.at[at(r, total // nr)], chat.at[at(r, total // nr)], s_c3, r_c3, sib)
    per = total // nr // TILE
    fb = fhat[...].astype(bf16)

    def scores(base):
        @pl.loop(0, per)
        def _(k):
            where = at(base * per + k, TILE)
            expo[:, where] = SCALE * dot(fb, chat[where, :], 1, 1)

    scores(r)
    c3.wait_recv()
    scores(other)
    logits = expo[...]
    mask = (pos[...] == ids[...]).astype(f32)
    ex = jnp.exp(logits)
    picked = mask * logits
    expo[...] = ex
    rowsum = jnp.sum(ex, axis=1, keepdims=True)
    rowpos = jnp.sum(picked, axis=1, keepdims=True)
    stat[0, 0:1, :] = jnp.sum(ex, axis=0, keepdims=True)
    stat[0, 1:2, :] = jnp.sum(picked, axis=0, keepdims=True)
    x1 = go(stat.at[0], stat.at[1], s_x1, r_x1, sib)
    fig_out[at(c, mine), :] = jnp.broadcast_to(jnp.log(rowsum) - rowpos, (mine, 128))
    ct = [
        go(fig_out.at[at(c, mine)], fig_out.at[at(c, mine)], s_t.at[j], r_t.at[j], (d, r, col_of(j)))
        for j in range(1, nc)
    ]
    x1.wait_recv()
    stat[2] = stat[0] + stat[1]
    x2 = [
        go(stat.at[2], stat.at[3 + j], s_x2.at[j], r_x2.at[j], (d, r, col_of(j))) for j in range(1, nc)
    ]
    acc = stat[2]
    for j in range(1, nc):
        x2[j - 1].wait_recv()
        acc = acc + stat[3 + j]
    stat[3] = acc
    x3 = [
        go(stat.at[3], stat.at[3 + nc + j], s_x3.at[j], r_x3.at[j], (dp_of(j), r, c))
        for j in range(1, nd)
    ]
    for j in range(1, nd):
        x3[j - 1].wait_recv()
        acc = acc + stat[3 + nc + j]
    colsum = acc[0:1, :]
    cap_out[...] = jnp.log(colsum) - acc[1:2, :]
    ex = expo[...]
    dlog[...] = (ex / rowsum + ex / colsum - 2.0 * mask).astype(bf16)

    @pl.loop(0, emb // TILE)
    def _(k):
        dfh[:, at(k, TILE)] = SCALE * dot(dlog[...], chat[:, at(k, TILE)], 1, 0)

    fh = fhat[...]
    df = dfh[...]
    demb[at(c, mine), :] = (
        (df - fh * jnp.sum(fh * df, axis=1, keepdims=True)) * inv
    ).astype(bf16)
    cd = [
        go(demb.at[at(c, mine)], demb.at[at(c, mine)], s_d.at[j], r_d.at[j], (d, r, col_of(j)))
        for j in range(1, nc)
    ]
    for cp in cd:
        cp.wait_recv()

    def place(k, src, core):
        return dpre.at[k, at(src * nr + core, rows)]

    def upward(k, s):
        spot = place(k, d + 1 - s, r)
        return remote(spot, spot, s_up.at[s, k], r_up.at[s, k], (jnp.minimum(d + 1, nd - 1), r, c))

    def downward(k, s):
        spot = place(k, d - 1 + s, r)
        return remote(spot, spot, s_dn.at[s, k], r_dn.at[s, k], (jnp.maximum(d - 1, 0), r, c))

    def across(k, src, n):
        spot = place(k, src, r)
        return remote(spot, spot, s_sib.at[n, k], r_sib.at[n, k], sib)

    @pl.loop(0, tiles)
    def _(k):
        dh = dot(demb[...], w_out[at(k, TILE), :], 1, 1)
        dpre[k, at(d * nr + r, rows), :] = (dh * slope[:, at(k, TILE)]).astype(bf16)

        @pl.when(d + 1 < nd)
        def _():
            upward(k, 1).start()

        @pl.when(d > 0)
        def _():
            downward(k, 1).start()

        across(k, d, 0).start()

    for t in range(nd):
        both = dot(hidden[...], demb[:, t * nr * lanes : (t + 1) * nr * lanes], 0, 0)
        low, high = both[:, :lanes], both[:, lanes:]
        first = r == 0
        hsum[t] = jnp.where(first, low, high)
        head[t] = jnp.where(first, high, low).astype(bf16)
    ch = remote(head, hsib, s_h, r_h, sib)
    ch.start()

    cg = []
    for j in range(1, nd):
        source = lax.rem(d + nd - j, nd)
        ca[j - 1].wait_recv()
        cb[j - 1].wait_recv()
        cg.append(go(stage.at[source], slices.at[at(source * nr + r, rows)], s_g.at[j], r_g.at[j], sib))
    remote(stage.at[0], stage.at[0], s_g.at[0], r_g.at[0], sib).wait_recv()
    for cp in cg:
        cp.wait_recv()

    def product(src, fresh):
        @pl.loop(0, tiles)
        def _(k):
            both = at(src, nr * rows)
            value = dot(slices[both, :], dpre[k, both, :], 0, 0)
            if fresh:
                gwi[:, at(k, TILE)] = value
            else:
                gwi[:, at(k, TILE)] += value

    def from_sibling(n):
        @pl.loop(0, tiles)
        def _(k):
            across(k, d, n).wait_recv()

    ch.wait_recv()
    for t in range(nd):
        hsum[t] = hsum[t] + hsib[t].astype(f32)

    def hop(t, buf, send, recv, nxt):
        return remote(head.at[t], buf.at[t], send.at[t], recv.at[t], (nxt, r, c))

    def up_hop(t):
        return hop(t, hup, s_hu, r_hu, jnp.minimum(d + 1, nd - 1))

    def dn_hop(t):
        return hop(t, hdn, s_hd, r_hd, jnp.maximum(d - 1, 0))

    ch.wait_send()

    def send_heads():
        for t in reversed(range(nd)):
            @pl.when(d < t)
            def _():
                @pl.when(d == 0)
                def _():
                    head[t] = hsum[t].astype(bf16)

                @pl.when(d > 0)
                def _():
                    up_hop(t).wait_recv()
                    head[t] = (hsum[t] + hup[t].astype(f32)).astype(bf16)

                up_hop(t).start()

        for t in range(nd):
            @pl.when(d > t)
            def _():
                @pl.when(d == nd - 1)
                def _():
                    head[t] = hsum[t].astype(bf16)

                @pl.when(d < nd - 1)
                def _():
                    dn_hop(t).wait_recv()
                    head[t] = (hsum[t] + hdn[t].astype(f32)).astype(bf16)

                dn_hop(t).start()

    def relay(s):
        @pl.loop(0, tiles)
        def _(k):
            @pl.when(d - s >= 0)
            def _():
                upward(k, s).wait_recv()

                @pl.when(d + 1 < nd)
                def _():
                    upward(k, s + 1).start()

                across(k, d - s, 2 * s - 1).start()

            @pl.when(d + s < nd)
            def _():
                downward(k, s).wait_recv()

                @pl.when(d > 0)
                def _():
                    downward(k, s + 1).start()

                across(k, d + s, 2 * s).start()

    def products(s):
        @pl.when(d - s >= 0)
        def _():
            from_sibling(2 * s - 1)
            product(d - s, False)

        @pl.when(d + s < nd)
        def _():
            from_sibling(2 * s)
            product(d + s, False)

    from_sibling(0)
    product(d, True)
    for s in range(1, nd):
        relay(s)
        if s == 1:
            send_heads()
        products(s)

    gwo[...] = hsum[d]

    @pl.when(d > 0)
    def _():
        up_hop(d).wait_recv()
        gwo[...] += hup[d].astype(f32)

    @pl.when(d < nd - 1)
    def _():
        dn_hop(d).wait_recv()
        gwo[...] += hdn[d].astype(f32)

    for cp in ct:
        cp.wait_recv()
    for cp in sent:
        cp.wait_send()
    for t in range(nd):
        @pl.when(d < t)
        def _():
            up_hop(t).wait_send()

        @pl.when(d > t)
        def _():
            dn_hop(t).wait_send()

    @pl.loop(0, tiles)
    def _(k):
        across(k, d, 0).wait_send()
        for s in range(1, nd + 1):
            if s < nd:
                @pl.when(d - s >= 0)
                def _():
                    across(k, d - s, 2 * s - 1).wait_send()

                @pl.when(d + s < nd)
                def _():
                    across(k, d + s, 2 * s).wait_send()

            @pl.when((d + 1 < nd) & (d + 1 - s >= 0))
            def _():
                upward(k, s).wait_send()

            @pl.when((d > 0) & (d - 1 + s < nd))
            def _():
                downward(k, s).wait_send()


def joined(features, w_in, w_out, captions, positive):
    nd, nr, nc = (lax.axis_size(a) for a in ("dp", "row", "col"))
    d, r, c = (lax.axis_index(a) for a in ("dp", "row", "col"))
    rows, din = features.shape
    half, hid = w_in.shape
    emb = w_out.shape[1]
    cap = captions.shape[0]
    mine = rows // nc
    total = nd * nr * nc * cap
    width, lanes = din // (nd * nr), emb // (nd * nr)
    tiles = hid // TILE
    pos = lax.dynamic_slice_in_dim(positive, c * mine, mine, 0)[:, None]
    ids = jnp.arange(total, dtype=jnp.int32).reshape(nd, nr, nc, cap)
    ids = ids.transpose(1, 2, 0, 3).reshape(1, total)
    f32, bf16 = jnp.float32, jnp.bfloat16
    V, D = pltpu.VMEM, pltpu.SemaphoreType.DMA
    one = D(())
    scratch = [
        V((rows, half), bf16), V((tiles, rows, TILE), f32), V((tiles, rows, TILE), f32),
        V((rows, hid), f32), V((rows, hid), f32), V((rows, hid), bf16), V((rows, emb), f32),
        V((nc, mine, emb), bf16), V((nc, mine, emb), bf16), V((mine, emb), f32),
        V((total, emb), bf16), V((mine, total), f32), V((mine, total), bf16),
        V((mine, emb), f32), V((rows, emb), bf16), V((tiles, nd * nr * rows, TILE), bf16),
        V((nd * nr * rows, width), bf16), V((nd, rows, width), bf16),
        V((3 + nc + nd, 2, total), f32),
        V((nd, hid, lanes), bf16), V((nd, hid, lanes), f32), V((nd, hid, lanes), bf16),
        V((nd, hid, lanes), bf16), V((nd, hid, lanes), bf16),
    ]
    sems = [
        one, D((tiles,)), D((nd,)), D((nc,)), one, D((nc,)),
        one, D((nc,)), D((nd,)), D((nc,)), D((nc,)),
        D((nd,)), D((nd,)), D((nd,)), D((nd + 1, tiles)), D((nd + 1, tiles)), D((2 * nd, tiles)),
        one, D((nd,)), D((nd,)),
    ]
    scratch += [s for s in sems for _ in range(2)]
    fig, capt, gwi, gwo = pl.pallas_call(
        functools.partial(kernel, nd, nr, nc),
        out_shape=(
            jax.ShapeDtypeStruct((rows, 128), f32),
            jax.ShapeDtypeStruct((1, total), f32),
            jax.ShapeDtypeStruct((width, hid), f32),
            jax.ShapeDtypeStruct((hid, lanes), f32),
        ),
        in_specs=[pl.BlockSpec(memory_space=V)] * 6,
        out_specs=[pl.BlockSpec(memory_space=V)] * 4,
        scratch_shapes=scratch,
        compiler_params=pltpu.CompilerParams(
            collective_id=0, has_side_effects=True, vmem_limit_bytes=60 * 2**20
        ),
    )(features, w_in, w_out, captions, pos, ids)
    slot = (r * nc + c) * nd + d
    cap_terms = lax.dynamic_slice_in_dim(capt[0], slot * cap, cap, 0)
    return fig[:, 0], cap_terms, gwi, gwo


def on_device(features, w_in, w_out, captions, positive):
    nd, nr, nc = (lax.axis_size(a) for a in ("dp", "row", "col"))
    groups = nd * nr
    small = groups * features.shape[0] <= 2048 and nr == 2 and nd > 1 and nc > 1
    even = features.shape[1] % (128 * groups) == 0 and w_out.shape[1] % (128 * groups) == 0
    body = joined if small and even else plain
    return body(features, w_in, w_out, captions, positive)


def solution(mesh):
    placed = (
        P(("dp", "row"), None),
        P("row", "col"),
        P("col", None),
        P(("dp", "row", "col"), None),
        P(("dp", "row")),
    )
    return jax.shard_map(
        on_device,
        mesh=mesh,
        in_specs=placed,
        out_specs=(
            P(("dp", "row")),
            P(("dp", "row", "col")),
            P(("dp", "row"), "col"),
            P("col", ("dp", "row")),
        ),
        check_vma=False,
    )
```

```python
import functools

import jax
import jax.numpy as jnp
from jax import lax
from jax.experimental import pallas as pl
from jax.experimental.pallas import tpu as pltpu
from jax.sharding import PartitionSpec as P

SCALE = 50.0
EPS = 1e-06


def gelu_back(pre, grad):
    return jax.vjp(jax.nn.gelu, pre)[1](grad)[0]


def plain(features, w_in, w_out, captions, positive):
    group = ("dp", "row")
    every = ("dp", "row", "col")
    f32 = jnp.float32
    slices = lax.all_to_all(features, group, 1, 0, tiled=True)
    cap32 = captions.astype(f32)
    chat_local = (cap32 * lax.rsqrt(jnp.sum(cap32 * cap32, axis=1, keepdims=True) + EPS)).astype(
        jnp.bfloat16
    )
    chat = lax.all_gather(chat_local, every, axis=0, tiled=True)
    pre = jnp.dot(
        features, lax.all_gather(w_in, "row", axis=0, tiled=True), preferred_element_type=f32
    )
    hidden = jax.nn.gelu(pre).astype(jnp.bfloat16)
    part = jnp.dot(hidden, w_out, preferred_element_type=f32)
    emb = lax.psum_scatter(part, "col", scatter_dimension=0, tiled=True)
    mine = emb.shape[0]
    inv = lax.rsqrt(jnp.sum(emb * emb, axis=1, keepdims=True) + EPS)
    fhat = emb * inv
    fhat_b = fhat.astype(jnp.bfloat16)
    logits = SCALE * lax.dot_general(
        fhat_b, chat, (((1,), (1,)), ((), ())), preferred_element_type=f32
    )
    col = lax.axis_index("col")
    places = lax.dynamic_slice_in_dim(positive, col * mine, mine, 0)
    colids = jnp.arange(chat.shape[0], dtype=jnp.int32)
    mask = (places[:, None] == colids[None, :]).astype(f32)
    expo = jnp.exp(logits)
    picked = mask * logits
    rowsum, rowpos = jnp.sum(expo, axis=1), jnp.sum(picked, axis=1)
    colsum, colpos = lax.psum((jnp.sum(expo, axis=0), jnp.sum(picked, axis=0)), every)
    fig_terms = lax.all_gather(jnp.log(rowsum) - rowpos, "col", axis=0, tiled=True)
    capdev = captions.shape[0]
    place = (lax.axis_index("dp") * lax.axis_size("row") + lax.axis_index("row")) * lax.axis_size(
        "col"
    ) + col
    cap_terms = lax.dynamic_slice_in_dim(jnp.log(colsum) - colpos, place * capdev, capdev, 0)
    dlog = (expo / rowsum[:, None] + expo / colsum[None, :] - 2.0 * mask).astype(jnp.bfloat16)
    dfhat = SCALE * jnp.dot(dlog, chat, preferred_element_type=f32)
    demb = ((dfhat - fhat * jnp.sum(fhat * dfhat, axis=1, keepdims=True)) * inv).astype(
        jnp.bfloat16
    )
    demb = lax.all_gather(demb, "col", axis=0, tiled=True)
    dh = lax.dot_general(demb, w_out, (((1,), (1,)), ((), ())), preferred_element_type=f32)
    dpre = gelu_back(pre, dh).astype(jnp.bfloat16)
    dpre_all = lax.all_gather(dpre, group, axis=0, tiled=True)
    head_term = lax.dot_general(
        hidden, demb, (((0,), (0,)), ((), ())), preferred_element_type=f32
    )
    grad_w_out = lax.psum_scatter(head_term, group, scatter_dimension=1, tiled=True)
    grad_w_in = lax.dot_general(
        slices, dpre_all, (((0,), (0,)), ((), ())), preferred_element_type=f32
    )
    return (fig_terms, cap_terms, grad_w_in, grad_w_out)


MESH = pl.DeviceIdType.MESH
ROOT = 0.7978845608028654
CUBE = 0.044715
TILE = 256


def gelu_and_slope(x):
    t = jnp.tanh(ROOT * (x + CUBE * x * x * x))
    half = 0.5 * (1.0 + t)
    return x * half, half + 0.5 * x * (1.0 - t * t) * (ROOT * (1.0 + 3.0 * CUBE * x * x))


def remote(src, dst, send, recv, where):
    return pltpu.make_async_remote_copy(
        src_ref=src, dst_ref=dst, send_sem=send, recv_sem=recv, device_id=where, device_id_type=MESH
    )


def dot(a, b, ca, cb):
    return lax.dot_general(a, b, (((ca,), (cb,)), ((), ())), preferred_element_type=jnp.float32)


def kernel(nd, nr, nc, feat, w_in, w_out, caps, pos, ids,
           fig_out, cap_out, gwi, gwo,
           fsib, psend, precv, pre, slope, hidden, part, esend, erecv, fhat, chat, expo, dlog,
           dfh, demb, dpre, slices, stage, stat, head, hsum, hsib, hup, hdn,
           s_f, r_f, s_p, r_p, s_c1, r_c1, s_c2, r_c2, s_c3, r_c3, s_e, r_e,
           s_x1, r_x1, s_x2, r_x2, s_x3, r_x3, s_d, r_d, s_t, r_t,
           s_a, r_a, s_b, r_b, s_g, r_g, s_q, r_q, s_up, r_up, s_dn, r_dn, s_sib, r_sib,
           s_h, r_h, s_hu, r_hu, s_hd, r_hd):
    f32, bf16 = jnp.float32, jnp.bfloat16
    d, r, c = lax.axis_index("dp"), lax.axis_index("row"), lax.axis_index("col")
    other = 1 - r
    sib = (d, other, c)
    rows = feat.shape[0]
    half = w_in.shape[0]
    hid = w_in.shape[1]
    emb = w_out.shape[1]
    mine = rows // nc
    cap = caps.shape[0]
    total = chat.shape[0]
    width = gwi.shape[0]
    lanes = gwo.shape[1]
    tiles = hid // TILE

    def col_of(j):
        return lax.rem(c + j, nc)

    def dp_of(j):
        return lax.rem(d + j, nd)

    def at(index, size):
        return pl.ds(pl.multiple_of(index * size, size), size)

    barrier = pltpu.get_barrier_semaphore()
    pl.semaphore_signal(barrier, inc=1, device_id=sib, device_id_type=MESH)
    for j in range(1, nc):
        pl.semaphore_signal(barrier, inc=1, device_id=(d, r, col_of(j)), device_id_type=MESH)
    for j in range(1, nd):
        pl.semaphore_signal(barrier, inc=1, device_id=(dp_of(j), r, c), device_id_type=MESH)
    pl.semaphore_wait(barrier, nc + nd - 1)
    sent = []

    def go(*a):
        cp = remote(*a)
        cp.start()
        sent.append(cp)
        return cp

    cf = go(feat.at[:, at(other, half)], fsib, s_f, r_f, sib)
    cap32 = caps[...].astype(f32)
    slot = (r * nc + c) * nd + d
    chat[at(slot, cap), :] = (
        cap32 * lax.rsqrt(jnp.sum(cap32 * cap32, axis=1, keepdims=True) + EPS)
    ).astype(bf16)
    c1 = [
        go(chat.at[at(slot, cap)], chat.at[at(slot, cap)], s_c1.at[j], r_c1.at[j], (dp_of(j), r, c))
        for j in range(1, nd)
    ]
    c2 = [[
        go(chat.at[at(slot, cap)], chat.at[at(slot, cap)], s_c2.at[j, 0], r_c2.at[j, 0], (d, r, col_of(j)))
        for j in range(1, nc)
    ]]
    mark = at(d * nr + r, rows)
    slices[mark, :] = feat[:, at(d * nr + r, width)]

    @pl.loop(0, tiles)
    def _(k):
        pre[:, at(k, TILE)] = dot(feat[:, at(r, half)], w_in[:, at(k, TILE)], 1, 0)

    cf.wait_recv()

    @pl.loop(0, tiles)
    def _(k):
        psend[k] = dot(fsib[...], w_in[:, at(k, TILE)], 1, 0)
        remote(psend.at[k], precv.at[k], s_p.at[k], r_p.at[k], sib).start()

    @pl.loop(0, tiles)
    def _(k):
        remote(psend.at[k], precv.at[k], s_p.at[k], r_p.at[k], sib).wait()
        x = pre[:, at(k, TILE)] + precv[k]
        pre[:, at(k, TILE)] = x
        hidden[:, at(k, TILE)] = gelu_and_slope(x)[0].astype(bf16)

    for i in range(1, nd):
        c1[i - 1].wait_recv()
        got = at((r * nc + c) * nd + lax.rem(d + nd - i, nd), cap)
        c2.append([
            go(chat.at[got], chat.at[got], s_c2.at[j, i], r_c2.at[j, i], (d, r, col_of(j)))
            for j in range(1, nc)
        ])

    def line(core, j):
        return at(core * nc + lax.rem(c + nc - j, nc), nd * cap)

    own = line(r, 0)
    c3 = [go(chat.at[own], chat.at[own], s_c3.at[0], r_c3.at[0], sib)]
    quarter = at(c, mine)
    ca, cb = [], []
    for j in range(1, nd):
        to = dp_of(j)
        ca.append(go(feat.at[quarter, at(to * nr + r, width)],
                     slices.at[at((d * nr + r) * nc + c, mine)], s_a.at[j], r_a.at[j], (to, r, c)))
        cb.append(go(feat.at[quarter, at(to * nr + other, width)],
                     stage.at[d], s_b.at[j], r_b.at[j], (to, r, c)))
    go(feat.at[:, at(d * nr + other, width)], slices.at[mark], s_g.at[0], r_g.at[0], sib)

    @pl.loop(0, emb // TILE)
    def _(k):
        part[:, at(k, TILE)] = dot(hidden[...], w_out[:, at(k, TILE)], 1, 0)

    ce = []
    for j in range(1, nc):
        esend[j] = part[at(col_of(j), mine), :].astype(bf16)
        ce.append(go(esend.at[j], erecv.at[j], s_e.at[j], r_e.at[j], (d, r, col_of(j))))

    @pl.loop(0, tiles)
    def _(k):
        slope[:, at(k, TILE)] = gelu_and_slope(pre[:, at(k, TILE)])[1]

    e = part[at(c, mine), :]
    for j in range(1, nc):
        ce[j - 1].wait_recv()
        e = e + erecv[j].astype(f32)
    inv = lax.rsqrt(jnp.sum(e * e, axis=1, keepdims=True) + EPS)
    fhat[...] = e * inv
    fb = fhat[...].astype(bf16)

    def scores(where):
        expo[:, where] = SCALE * dot(fb, chat[where, :], 1, 1)

    scores(own)
    for j in range(1, nc):
        for i in range(nd):
            c2[i][j - 1].wait_recv()
        c3.append(go(chat.at[line(r, j)], chat.at[line(r, j)], s_c3.at[j], r_c3.at[j], sib))
        scores(line(r, j))
    for j in range(nc):
        c3[j].wait_recv()
        scores(line(other, j))
    logits = expo[...]
    mask = (pos[...] == ids[...]).astype(f32)
    ex = jnp.exp(logits)
    picked = mask * logits
    expo[...] = ex
    rowsum = jnp.sum(ex, axis=1, keepdims=True)
    rowpos = jnp.sum(picked, axis=1, keepdims=True)
    stat[0, 0:1, :] = jnp.sum(ex, axis=0, keepdims=True)
    stat[0, 1:2, :] = jnp.sum(picked, axis=0, keepdims=True)
    x1 = go(stat.at[0], stat.at[1], s_x1, r_x1, sib)
    fig_out[at(c, mine), :] = jnp.broadcast_to(jnp.log(rowsum) - rowpos, (mine, 128))
    ct = [
        go(fig_out.at[at(c, mine)], fig_out.at[at(c, mine)], s_t.at[j], r_t.at[j], (d, r, col_of(j)))
        for j in range(1, nc)
    ]
    x1.wait_recv()
    stat[2] = stat[0] + stat[1]
    x2 = [
        go(stat.at[2], stat.at[3 + j], s_x2.at[j], r_x2.at[j], (d, r, col_of(j))) for j in range(1, nc)
    ]
    acc = stat[2]
    for j in range(1, nc):
        x2[j - 1].wait_recv()
        acc = acc + stat[3 + j]
    stat[3] = acc
    x3 = [
        go(stat.at[3], stat.at[3 + nc + j], s_x3.at[j], r_x3.at[j], (dp_of(j), r, c))
        for j in range(1, nd)
    ]
    for j in range(1, nd):
        x3[j - 1].wait_recv()
        acc = acc + stat[3 + nc + j]
    colsum = acc[0:1, :]
    cap_out[...] = jnp.log(colsum) - acc[1:2, :]
    ex = expo[...]
    dlog[...] = (ex / rowsum + ex / colsum - 2.0 * mask).astype(bf16)

    @pl.loop(0, emb // TILE)
    def _(k):
        dfh[:, at(k, TILE)] = SCALE * dot(dlog[...], chat[:, at(k, TILE)], 1, 0)

    fh = fhat[...]
    df = dfh[...]
    demb[at(c, mine), :] = (
        (df - fh * jnp.sum(fh * df, axis=1, keepdims=True)) * inv
    ).astype(bf16)
    cd = [
        go(demb.at[at(c, mine)], demb.at[at(c, mine)], s_d.at[j], r_d.at[j], (d, r, col_of(j)))
        for j in range(1, nc)
    ]
    for cp in cd:
        cp.wait_recv()

    def place(k, src, core):
        return dpre.at[k, at(src * nr + core, rows)]

    def upward(k, s):
        spot = place(k, d + 1 - s, r)
        return remote(spot, spot, s_up.at[s, k], r_up.at[s, k], (jnp.minimum(d + 1, nd - 1), r, c))

    def downward(k, s):
        spot = place(k, d - 1 + s, r)
        return remote(spot, spot, s_dn.at[s, k], r_dn.at[s, k], (jnp.maximum(d - 1, 0), r, c))

    def across(k, src, n):
        spot = place(k, src, r)
        return remote(spot, spot, s_sib.at[n, k], r_sib.at[n, k], sib)

    @pl.loop(0, tiles)
    def _(k):
        dh = dot(demb[...], w_out[at(k, TILE), :], 1, 1)
        dpre[k, at(d * nr + r, rows), :] = (dh * slope[:, at(k, TILE)]).astype(bf16)

        @pl.when(d + 1 < nd)
        def _():
            upward(k, 1).start()

        @pl.when(d > 0)
        def _():
            downward(k, 1).start()

        across(k, d, 0).start()

    for t in range(nd):
        both = dot(hidden[...], demb[:, t * nr * lanes : (t + 1) * nr * lanes], 0, 0)
        low, high = both[:, :lanes], both[:, lanes:]
        first = r == 0
        hsum[t] = jnp.where(first, low, high)
        head[t] = jnp.where(first, high, low).astype(bf16)
    ch = remote(head, hsib, s_h, r_h, sib)
    ch.start()

    def share(source, core, n):
        spot = at((source * nr + core) * nc + c, mine)
        return [
            go(slices.at[spot], slices.at[spot], s_q.at[q, n], r_q.at[q, n], (d, r, col_of(q)))
            for q in range(1, nc)
        ]

    cg, cq = [], []
    for j in range(1, nd):
        source = lax.rem(d + nd - j, nd)
        ca[j - 1].wait_recv()
        cb[j - 1].wait_recv()
        spot = at((source * nr + r) * nc + c, mine)
        cg.append(go(stage.at[source], slices.at[spot], s_g.at[j], r_g.at[j], sib))
        cq += share(source, r, j)
    for j in range(1, nd):
        cg[j - 1].wait_recv()
        cq += share(lax.rem(d + nd - j, nd), other, nd + j)
    remote(slices.at[mark], slices.at[mark], s_g.at[0], r_g.at[0], sib).wait_recv()

    def product(src, fresh):
        @pl.loop(0, tiles)
        def _(k):
            both = at(src, nr * rows)
            value = dot(slices[both, :], dpre[k, both, :], 0, 0)
            if fresh:
                gwi[:, at(k, TILE)] = value
            else:
                gwi[:, at(k, TILE)] += value

    def from_sibling(n):
        @pl.loop(0, tiles)
        def _(k):
            across(k, d, n).wait_recv()

    ch.wait_recv()
    for t in range(nd):
        hsum[t] = hsum[t] + hsib[t].astype(f32)

    def hop(t, buf, send, recv, nxt):
        return remote(head.at[t], buf.at[t], send.at[t], recv.at[t], (nxt, r, c))

    def up_hop(t):
        return hop(t, hup, s_hu, r_hu, jnp.minimum(d + 1, nd - 1))

    def dn_hop(t):
        return hop(t, hdn, s_hd, r_hd, jnp.maximum(d - 1, 0))

    ch.wait_send()

    def send_heads():
        for t in reversed(range(nd)):
            @pl.when(d < t)
            def _():
                @pl.when(d == 0)
                def _():
                    head[t] = hsum[t].astype(bf16)

                @pl.when(d > 0)
                def _():
                    up_hop(t).wait_recv()
                    head[t] = (hsum[t] + hup[t].astype(f32)).astype(bf16)

                up_hop(t).start()

        for t in range(nd):
            @pl.when(d > t)
            def _():
                @pl.when(d == nd - 1)
                def _():
                    head[t] = hsum[t].astype(bf16)

                @pl.when(d < nd - 1)
                def _():
                    dn_hop(t).wait_recv()
                    head[t] = (hsum[t] + hdn[t].astype(f32)).astype(bf16)

                dn_hop(t).start()

    def relay(s):
        @pl.loop(0, tiles)
        def _(k):
            @pl.when(d - s >= 0)
            def _():
                upward(k, s).wait_recv()

                @pl.when(d + 1 < nd)
                def _():
                    upward(k, s + 1).start()

                across(k, d - s, 2 * s - 1).start()

            @pl.when(d + s < nd)
            def _():
                downward(k, s).wait_recv()

                @pl.when(d > 0)
                def _():
                    downward(k, s + 1).start()

                across(k, d + s, 2 * s).start()

    def products(s):
        @pl.when(d - s >= 0)
        def _():
            from_sibling(2 * s - 1)
            product(d - s, False)

        @pl.when(d + s < nd)
        def _():
            from_sibling(2 * s)
            product(d + s, False)

    from_sibling(0)
    product(d, True)
    for s in range(1, nd):
        relay(s)
        if s == 1:
            send_heads()
            for cp in cq:
                cp.wait_recv()
        products(s)

    gwo[...] = hsum[d]

    @pl.when(d > 0)
    def _():
        up_hop(d).wait_recv()
        gwo[...] += hup[d].astype(f32)

    @pl.when(d < nd - 1)
    def _():
        dn_hop(d).wait_recv()
        gwo[...] += hdn[d].astype(f32)

    for cp in ct:
        cp.wait_recv()
    for cp in sent:
        cp.wait_send()
    for t in range(nd):
        @pl.when(d < t)
        def _():
            up_hop(t).wait_send()

        @pl.when(d > t)
        def _():
            dn_hop(t).wait_send()

    @pl.loop(0, tiles)
    def _(k):
        across(k, d, 0).wait_send()
        for s in range(1, nd + 1):
            if s < nd:
                @pl.when(d - s >= 0)
                def _():
                    across(k, d - s, 2 * s - 1).wait_send()

                @pl.when(d + s < nd)
                def _():
                    across(k, d + s, 2 * s).wait_send()

            @pl.when((d + 1 < nd) & (d + 1 - s >= 0))
            def _():
                upward(k, s).wait_send()

            @pl.when((d > 0) & (d - 1 + s < nd))
            def _():
                downward(k, s).wait_send()


def joined(features, w_in, w_out, captions, positive):
    nd, nr, nc = (lax.axis_size(a) for a in ("dp", "row", "col"))
    d, r, c = (lax.axis_index(a) for a in ("dp", "row", "col"))
    rows, din = features.shape
    half, hid = w_in.shape
    emb = w_out.shape[1]
    cap = captions.shape[0]
    mine = rows // nc
    total = nd * nr * nc * cap
    width, lanes = din // (nd * nr), emb // (nd * nr)
    tiles = hid // TILE
    pos = lax.dynamic_slice_in_dim(positive, c * mine, mine, 0)[:, None]
    ids = jnp.arange(total, dtype=jnp.int32).reshape(nd, nr, nc, cap)
    ids = ids.transpose(1, 2, 0, 3).reshape(1, total)
    f32, bf16 = jnp.float32, jnp.bfloat16
    V, D = pltpu.VMEM, pltpu.SemaphoreType.DMA
    one = D(())
    scratch = [
        V((rows, half), bf16), V((tiles, rows, TILE), f32), V((tiles, rows, TILE), f32),
        V((rows, hid), f32), V((rows, hid), f32), V((rows, hid), bf16), V((rows, emb), f32),
        V((nc, mine, emb), bf16), V((nc, mine, emb), bf16), V((mine, emb), f32),
        V((total, emb), bf16), V((mine, total), f32), V((mine, total), bf16),
        V((mine, emb), f32), V((rows, emb), bf16), V((tiles, nd * nr * rows, TILE), bf16),
        V((nd * nr * rows, width), bf16), V((nd, mine, width), bf16),
        V((3 + nc + nd, 2, total), f32),
        V((nd, hid, lanes), bf16), V((nd, hid, lanes), f32), V((nd, hid, lanes), bf16),
        V((nd, hid, lanes), bf16), V((nd, hid, lanes), bf16),
    ]
    sems = [
        one, D((tiles,)), D((nd,)), D((nc, nd)), D((nc,)), D((nc,)),
        one, D((nc,)), D((nd,)), D((nc,)), D((nc,)),
        D((nd,)), D((nd,)), D((nd,)), D((nc, 2 * nd)), D((nd + 1, tiles)), D((nd + 1, tiles)), D((2 * nd, tiles)),
        one, D((nd,)), D((nd,)),
    ]
    scratch += [s for s in sems for _ in range(2)]
    fig, capt, gwi, gwo = pl.pallas_call(
        functools.partial(kernel, nd, nr, nc),
        out_shape=(
            jax.ShapeDtypeStruct((rows, 128), f32),
            jax.ShapeDtypeStruct((1, total), f32),
            jax.ShapeDtypeStruct((width, hid), f32),
            jax.ShapeDtypeStruct((hid, lanes), f32),
        ),
        in_specs=[pl.BlockSpec(memory_space=V)] * 6,
        out_specs=[pl.BlockSpec(memory_space=V)] * 4,
        scratch_shapes=scratch,
        compiler_params=pltpu.CompilerParams(
            collective_id=0, has_side_effects=True, vmem_limit_bytes=60 * 2**20
        ),
    )(features, w_in, w_out, captions, pos, ids)
    slot = (r * nc + c) * nd + d
    cap_terms = lax.dynamic_slice_in_dim(capt[0], slot * cap, cap, 0)
    return fig[:, 0], cap_terms, gwi, gwo


def on_device(features, w_in, w_out, captions, positive):
    nd, nr, nc = (lax.axis_size(a) for a in ("dp", "row", "col"))
    groups = nd * nr
    small = groups * features.shape[0] <= 2048 and nr == 2 and nd > 1 and nc > 1
    even = (nd * captions.shape[0]) % 128 == 0 and features.shape[1] % (128 * groups) == 0 and w_out.shape[1] % (128 * groups) == 0
    body = joined if small and even else plain
    return body(features, w_in, w_out, captions, positive)


def solution(mesh):
    placed = (
        P(("dp", "row"), None),
        P("row", "col"),
        P("col", None),
        P(("dp", "row", "col"), None),
        P(("dp", "row")),
    )
    return jax.shard_map(
        on_device,
        mesh=mesh,
        in_specs=placed,
        out_specs=(
            P(("dp", "row")),
            P(("dp", "row", "col")),
            P(("dp", "row"), "col"),
            P("col", ("dp", "row")),
        ),
        check_vma=False,
    )
```

```python
import functools

import jax
import jax.numpy as jnp
from jax import lax
from jax.experimental import pallas as pl
from jax.experimental.pallas import tpu as pltpu
from jax.sharding import PartitionSpec as P

SCALE = 50.0
EPS = 1e-06


def gelu_back(pre, grad):
    return jax.vjp(jax.nn.gelu, pre)[1](grad)[0]


def plain(features, w_in, w_out, captions, positive):
    group = ("dp", "row")
    every = ("dp", "row", "col")
    f32 = jnp.float32
    slices = lax.all_to_all(features, group, 1, 0, tiled=True)
    cap32 = captions.astype(f32)
    chat_local = (cap32 * lax.rsqrt(jnp.sum(cap32 * cap32, axis=1, keepdims=True) + EPS)).astype(
        jnp.bfloat16
    )
    chat = lax.all_gather(chat_local, every, axis=0, tiled=True)
    pre = jnp.dot(
        features, lax.all_gather(w_in, "row", axis=0, tiled=True), preferred_element_type=f32
    )
    hidden = jax.nn.gelu(pre).astype(jnp.bfloat16)
    part = jnp.dot(hidden, w_out, preferred_element_type=f32)
    emb = lax.psum_scatter(part, "col", scatter_dimension=0, tiled=True)
    mine = emb.shape[0]
    inv = lax.rsqrt(jnp.sum(emb * emb, axis=1, keepdims=True) + EPS)
    fhat = emb * inv
    fhat_b = fhat.astype(jnp.bfloat16)
    logits = SCALE * lax.dot_general(
        fhat_b, chat, (((1,), (1,)), ((), ())), preferred_element_type=f32
    )
    col = lax.axis_index("col")
    places = lax.dynamic_slice_in_dim(positive, col * mine, mine, 0)
    colids = jnp.arange(chat.shape[0], dtype=jnp.int32)
    mask = (places[:, None] == colids[None, :]).astype(f32)
    expo = jnp.exp(logits)
    picked = mask * logits
    rowsum, rowpos = jnp.sum(expo, axis=1), jnp.sum(picked, axis=1)
    colsum, colpos = lax.psum((jnp.sum(expo, axis=0), jnp.sum(picked, axis=0)), every)
    fig_terms = lax.all_gather(jnp.log(rowsum) - rowpos, "col", axis=0, tiled=True)
    capdev = captions.shape[0]
    place = (lax.axis_index("dp") * lax.axis_size("row") + lax.axis_index("row")) * lax.axis_size(
        "col"
    ) + col
    cap_terms = lax.dynamic_slice_in_dim(jnp.log(colsum) - colpos, place * capdev, capdev, 0)
    dlog = (expo / rowsum[:, None] + expo / colsum[None, :] - 2.0 * mask).astype(jnp.bfloat16)
    dfhat = SCALE * jnp.dot(dlog, chat, preferred_element_type=f32)
    demb = ((dfhat - fhat * jnp.sum(fhat * dfhat, axis=1, keepdims=True)) * inv).astype(
        jnp.bfloat16
    )
    demb = lax.all_gather(demb, "col", axis=0, tiled=True)
    dh = lax.dot_general(demb, w_out, (((1,), (1,)), ((), ())), preferred_element_type=f32)
    dpre = gelu_back(pre, dh).astype(jnp.bfloat16)
    dpre_all = lax.all_gather(dpre, group, axis=0, tiled=True)
    head_term = lax.dot_general(
        hidden, demb, (((0,), (0,)), ((), ())), preferred_element_type=f32
    )
    grad_w_out = lax.psum_scatter(head_term, group, scatter_dimension=1, tiled=True)
    grad_w_in = lax.dot_general(
        slices, dpre_all, (((0,), (0,)), ((), ())), preferred_element_type=f32
    )
    return (fig_terms, cap_terms, grad_w_in, grad_w_out)


MESH = pl.DeviceIdType.MESH
ROOT = 0.7978845608028654
CUBE = 0.044715
TILE = 256


def gelu_and_slope(x):
    t = jnp.tanh(ROOT * (x + CUBE * x * x * x))
    half = 0.5 * (1.0 + t)
    return x * half, half + 0.5 * x * (1.0 - t * t) * (ROOT * (1.0 + 3.0 * CUBE * x * x))


def remote(src, dst, send, recv, where):
    return pltpu.make_async_remote_copy(
        src_ref=src, dst_ref=dst, send_sem=send, recv_sem=recv, device_id=where, device_id_type=MESH
    )


def dot(a, b, ca, cb):
    return lax.dot_general(a, b, (((ca,), (cb,)), ((), ())), preferred_element_type=jnp.float32)


def kernel(nd, nr, nc, feat, w_in, w_out, caps, pos, ids,
           fig_out, cap_out, gwi, gwo,
           fsib, psend, precv, pre, slope, hidden, part, esend, erecv, fhat, chat, expo, dlog,
           dfh, demb, dpre, slices, stage, stat, head, hsum, hsib, hup, hdn,
           s_f, r_f, s_p, r_p, s_c1, r_c1, s_c2, r_c2, s_c3, r_c3, s_e, r_e,
           s_x1, r_x1, s_x2, r_x2, s_x3, r_x3, s_d, r_d, s_t, r_t,
           s_a, r_a, s_b, r_b, s_g, r_g, s_q, r_q, s_up, r_up, s_dn, r_dn, s_sib, r_sib,
           s_h, r_h, s_hu, r_hu, s_hd, r_hd):
    f32, bf16 = jnp.float32, jnp.bfloat16
    d, r, c = lax.axis_index("dp"), lax.axis_index("row"), lax.axis_index("col")
    other = 1 - r
    sib = (d, other, c)
    rows = feat.shape[0]
    half = w_in.shape[0]
    hid = w_in.shape[1]
    emb = w_out.shape[1]
    mine = rows // nc
    cap = caps.shape[0]
    total = chat.shape[0]
    width = gwi.shape[0]
    lanes = gwo.shape[1]
    tiles = hid // TILE

    def col_of(j):
        return lax.rem(c + j, nc)

    def dp_of(j):
        return lax.rem(d + j, nd)

    def at(index, size):
        return pl.ds(pl.multiple_of(index * size, size), size)

    barrier = pltpu.get_barrier_semaphore()
    pl.semaphore_signal(barrier, inc=1, device_id=sib, device_id_type=MESH)
    for j in range(1, nc):
        pl.semaphore_signal(barrier, inc=1, device_id=(d, r, col_of(j)), device_id_type=MESH)
    for j in range(1, nd):
        pl.semaphore_signal(barrier, inc=1, device_id=(dp_of(j), r, c), device_id_type=MESH)
    pl.semaphore_wait(barrier, nc + nd - 1)
    sent = []

    def go(*a):
        cp = remote(*a)
        cp.start()
        sent.append(cp)
        return cp

    cf = go(feat.at[:, at(other, half)], fsib, s_f, r_f, sib)
    cap32 = caps[...].astype(f32)
    slot = (r * nc + c) * nd + d
    chat[at(slot, cap), :] = (
        cap32 * lax.rsqrt(jnp.sum(cap32 * cap32, axis=1, keepdims=True) + EPS)
    ).astype(bf16)
    c1 = [
        go(chat.at[at(slot, cap)], chat.at[at(slot, cap)], s_c1.at[j], r_c1.at[j], (dp_of(j), r, c))
        for j in range(1, nd)
    ]
    c2 = [[
        go(chat.at[at(slot, cap)], chat.at[at(slot, cap)], s_c2.at[j, 0], r_c2.at[j, 0], (d, r, col_of(j)))
        for j in range(1, nc)
    ]]
    mark = at(d * nr + r, rows)
    slices[mark, :] = feat[:, at(d * nr + r, width)]

    @pl.loop(0, tiles)
    def _(k):
        pre[:, at(k, TILE)] = dot(feat[:, at(r, half)], w_in[:, at(k, TILE)], 1, 0)

    cf.wait_recv()

    @pl.loop(0, tiles)
    def _(k):
        psend[k] = dot(fsib[...], w_in[:, at(k, TILE)], 1, 0)
        remote(psend.at[k], precv.at[k], s_p.at[k], r_p.at[k], sib).start()

    @pl.loop(0, tiles)
    def _(k):
        remote(psend.at[k], precv.at[k], s_p.at[k], r_p.at[k], sib).wait()
        x = pre[:, at(k, TILE)] + precv[k]
        pre[:, at(k, TILE)] = x
        hidden[:, at(k, TILE)] = gelu_and_slope(x)[0].astype(bf16)

    for i in range(1, nd):
        c1[i - 1].wait_recv()
        got = at((r * nc + c) * nd + lax.rem(d + nd - i, nd), cap)
        c2.append([
            go(chat.at[got], chat.at[got], s_c2.at[j, i], r_c2.at[j, i], (d, r, col_of(j)))
            for j in range(1, nc)
        ])

    def line(core, j):
        return at(core * nc + lax.rem(c + nc - j, nc), nd * cap)

    own = line(r, 0)
    c3 = [go(chat.at[own], chat.at[own], s_c3.at[0], r_c3.at[0], sib)]
    quarter = at(c, mine)
    ca, cb = [], []
    for j in range(1, nd):
        to = dp_of(j)
        ca.append(go(feat.at[quarter, at(to * nr + r, width)],
                     slices.at[at((d * nr + r) * nc + c, mine)], s_a.at[j], r_a.at[j], (to, r, c)))
        cb.append(go(feat.at[quarter, at(to * nr + other, width)],
                     stage.at[d], s_b.at[j], r_b.at[j], (to, r, c)))
    go(feat.at[:, at(d * nr + other, width)], slices.at[mark], s_g.at[0], r_g.at[0], sib)

    @pl.loop(0, emb // TILE)
    def _(k):
        part[:, at(k, TILE)] = dot(hidden[...], w_out[:, at(k, TILE)], 1, 0)

    ce = []
    for j in range(1, nc):
        esend[j] = part[at(col_of(j), mine), :].astype(bf16)
        ce.append(go(esend.at[j], erecv.at[j], s_e.at[j], r_e.at[j], (d, r, col_of(j))))

    @pl.loop(0, tiles)
    def _(k):
        slope[:, at(k, TILE)] = gelu_and_slope(pre[:, at(k, TILE)])[1]

    e = part[at(c, mine), :]
    for j in range(1, nc):
        ce[j - 1].wait_recv()
        e = e + erecv[j].astype(f32)
    inv = lax.rsqrt(jnp.sum(e * e, axis=1, keepdims=True) + EPS)
    fhat[...] = e * inv
    fb = fhat[...].astype(bf16)

    def scores(where):
        expo[:, where] = SCALE * dot(fb, chat[where, :], 1, 1)

    scores(own)
    for j in range(1, nc):
        for i in range(nd):
            c2[i][j - 1].wait_recv()
        c3.append(go(chat.at[line(r, j)], chat.at[line(r, j)], s_c3.at[j], r_c3.at[j], sib))
        scores(line(r, j))
    for j in range(nc):
        c3[j].wait_recv()
        scores(line(other, j))
    logits = expo[...]
    mask = (pos[...] == ids[...]).astype(f32)
    ex = jnp.exp(logits)
    picked = mask * logits
    expo[...] = ex
    rowsum = jnp.sum(ex, axis=1, keepdims=True)
    rowpos = jnp.sum(picked, axis=1, keepdims=True)
    stat[0, 0:1, :] = jnp.sum(ex, axis=0, keepdims=True)
    stat[0, 1:2, :] = jnp.sum(picked, axis=0, keepdims=True)
    x1 = go(stat.at[0], stat.at[1], s_x1, r_x1, sib)
    fig_out[at(c, mine), :] = jnp.broadcast_to(jnp.log(rowsum) - rowpos, (mine, 128))
    ct = [
        go(fig_out.at[at(c, mine)], fig_out.at[at(c, mine)], s_t.at[j], r_t.at[j], (d, r, col_of(j)))
        for j in range(1, nc)
    ]
    x1.wait_recv()
    stat[2] = stat[0] + stat[1]
    x2 = [
        go(stat.at[2], stat.at[3 + j], s_x2.at[j], r_x2.at[j], (d, r, col_of(j))) for j in range(1, nc)
    ]
    acc = stat[2]
    for j in range(1, nc):
        x2[j - 1].wait_recv()
        acc = acc + stat[3 + j]
    stat[3] = acc
    x3 = [
        go(stat.at[3], stat.at[3 + nc + j], s_x3.at[j], r_x3.at[j], (dp_of(j), r, c))
        for j in range(1, nd)
    ]
    for j in range(1, nd):
        x3[j - 1].wait_recv()
        acc = acc + stat[3 + nc + j]
    colsum = acc[0:1, :]
    cap_out[...] = jnp.log(colsum) - acc[1:2, :]
    ex = expo[...]
    dlog[...] = (ex / rowsum + ex / colsum - 2.0 * mask).astype(bf16)

    @pl.loop(0, emb // TILE)
    def _(k):
        dfh[:, at(k, TILE)] = SCALE * dot(dlog[...], chat[:, at(k, TILE)], 1, 0)

    fh = fhat[...]
    df = dfh[...]
    demb[at(c, mine), :] = (
        (df - fh * jnp.sum(fh * df, axis=1, keepdims=True)) * inv
    ).astype(bf16)
    cd = [
        go(demb.at[at(c, mine)], demb.at[at(c, mine)], s_d.at[j], r_d.at[j], (d, r, col_of(j)))
        for j in range(1, nc)
    ]
    for cp in cd:
        cp.wait_recv()

    def place(k, src, core):
        return dpre.at[k, at(src * nr + core, rows)]

    def upward(k, s):
        spot = place(k, d + 1 - s, r)
        return remote(spot, spot, s_up.at[s, k], r_up.at[s, k], (jnp.minimum(d + 1, nd - 1), r, c))

    def downward(k, s):
        spot = place(k, d - 1 + s, r)
        return remote(spot, spot, s_dn.at[s, k], r_dn.at[s, k], (jnp.maximum(d - 1, 0), r, c))

    def across(k, src, n):
        spot = place(k, src, r)
        return remote(spot, spot, s_sib.at[n, k], r_sib.at[n, k], sib)

    @pl.loop(0, tiles)
    def _(k):
        dh = dot(demb[...], w_out[at(k, TILE), :], 1, 1)
        dpre[k, at(d * nr + r, rows), :] = (dh * slope[:, at(k, TILE)]).astype(bf16)

        @pl.when(d + 1 < nd)
        def _():
            upward(k, 1).start()

        @pl.when(d > 0)
        def _():
            downward(k, 1).start()

        across(k, d, 0).start()

    for t in range(nd):
        both = dot(hidden[...], demb[:, t * nr * lanes : (t + 1) * nr * lanes], 0, 0)
        low, high = both[:, :lanes], both[:, lanes:]
        first = r == 0
        hsum[t] = jnp.where(first, low, high)
        head[t] = jnp.where(first, high, low).astype(bf16)
    ch = remote(head, hsib, s_h, r_h, sib)
    ch.start()

    def share(source, core, n):
        spot = at((source * nr + core) * nc + c, mine)
        return [
            go(slices.at[spot], slices.at[spot], s_q.at[q, n], r_q.at[q, n], (d, r, col_of(q)))
            for q in range(1, nc)
        ]

    cg, cq = [], []
    for j in range(1, nd):
        source = lax.rem(d + nd - j, nd)
        ca[j - 1].wait_recv()
        cb[j - 1].wait_recv()
        spot = at((source * nr + r) * nc + c, mine)
        cg.append(go(stage.at[source], slices.at[spot], s_g.at[j], r_g.at[j], sib))
        cq += share(source, r, j)
    for j in range(1, nd):
        cg[j - 1].wait_recv()
        cq += share(lax.rem(d + nd - j, nd), other, nd + j)
    remote(slices.at[mark], slices.at[mark], s_g.at[0], r_g.at[0], sib).wait_recv()

    def product(src, fresh):
        @pl.loop(0, tiles)
        def _(k):
            both = at(src, nr * rows)
            value = dot(slices[both, :], dpre[k, both, :], 0, 0)
            if fresh:
                gwi[:, at(k, TILE)] = value
            else:
                gwi[:, at(k, TILE)] += value

    def from_sibling(n):
        @pl.loop(0, tiles)
        def _(k):
            across(k, d, n).wait_recv()

    ch.wait_recv()
    for t in range(nd):
        hsum[t] = hsum[t] + hsib[t].astype(f32)

    def hop(t, buf, send, recv, nxt):
        return remote(head.at[t], buf.at[t], send.at[t], recv.at[t], (nxt, r, c))

    def up_hop(t):
        return hop(t, hup, s_hu, r_hu, jnp.minimum(d + 1, nd - 1))

    def dn_hop(t):
        return hop(t, hdn, s_hd, r_hd, jnp.maximum(d - 1, 0))

    ch.wait_send()

    for t in reversed(range(1, nd)):
        @pl.when(d == 0)
        def _():
            head[t] = hsum[t].astype(bf16)
            up_hop(t).start()

    for t in range(nd - 1):
        @pl.when(d == nd - 1)
        def _():
            head[t] = hsum[t].astype(bf16)
            dn_hop(t).start()

    def pass_heads():
        for t in reversed(range(nd)):
            @pl.when((d > 0) & (d < t))
            def _():
                up_hop(t).wait_recv()
                head[t] = (hsum[t] + hup[t].astype(f32)).astype(bf16)
                up_hop(t).start()

        for t in range(nd):
            @pl.when((d < nd - 1) & (d > t))
            def _():
                dn_hop(t).wait_recv()
                head[t] = (hsum[t] + hdn[t].astype(f32)).astype(bf16)
                dn_hop(t).start()

    def relay(s):
        @pl.loop(0, tiles)
        def _(k):
            @pl.when(d - s >= 0)
            def _():
                upward(k, s).wait_recv()

                @pl.when(d + 1 < nd)
                def _():
                    upward(k, s + 1).start()

                across(k, d - s, 2 * s - 1).start()

            @pl.when(d + s < nd)
            def _():
                downward(k, s).wait_recv()

                @pl.when(d > 0)
                def _():
                    downward(k, s + 1).start()

                across(k, d + s, 2 * s).start()

    def products(s):
        @pl.when(d - s >= 0)
        def _():
            from_sibling(2 * s - 1)
            product(d - s, False)

        @pl.when(d + s < nd)
        def _():
            from_sibling(2 * s)
            product(d + s, False)

    from_sibling(0)
    product(d, True)
    for s in range(1, nd - 1):
        relay(s)
    pass_heads()
    for cp in cq:
        cp.wait_recv()
    for s in range(1, nd - 1):
        products(s)
    relay(nd - 1)
    products(nd - 1)

    gwo[...] = hsum[d]

    @pl.when(d > 0)
    def _():
        up_hop(d).wait_recv()
        gwo[...] += hup[d].astype(f32)

    @pl.when(d < nd - 1)
    def _():
        dn_hop(d).wait_recv()
        gwo[...] += hdn[d].astype(f32)

    for cp in ct:
        cp.wait_recv()
    for cp in sent:
        cp.wait_send()
    for t in range(nd):
        @pl.when(d < t)
        def _():
            up_hop(t).wait_send()

        @pl.when(d > t)
        def _():
            dn_hop(t).wait_send()

    @pl.loop(0, tiles)
    def _(k):
        across(k, d, 0).wait_send()
        for s in range(1, nd + 1):
            if s < nd:
                @pl.when(d - s >= 0)
                def _():
                    across(k, d - s, 2 * s - 1).wait_send()

                @pl.when(d + s < nd)
                def _():
                    across(k, d + s, 2 * s).wait_send()

            @pl.when((d + 1 < nd) & (d + 1 - s >= 0))
            def _():
                upward(k, s).wait_send()

            @pl.when((d > 0) & (d - 1 + s < nd))
            def _():
                downward(k, s).wait_send()


def joined(features, w_in, w_out, captions, positive):
    nd, nr, nc = (lax.axis_size(a) for a in ("dp", "row", "col"))
    d, r, c = (lax.axis_index(a) for a in ("dp", "row", "col"))
    rows, din = features.shape
    half, hid = w_in.shape
    emb = w_out.shape[1]
    cap = captions.shape[0]
    mine = rows // nc
    total = nd * nr * nc * cap
    width, lanes = din // (nd * nr), emb // (nd * nr)
    tiles = hid // TILE
    pos = lax.dynamic_slice_in_dim(positive, c * mine, mine, 0)[:, None]
    ids = jnp.arange(total, dtype=jnp.int32).reshape(nd, nr, nc, cap)
    ids = ids.transpose(1, 2, 0, 3).reshape(1, total)
    f32, bf16 = jnp.float32, jnp.bfloat16
    V, D = pltpu.VMEM, pltpu.SemaphoreType.DMA
    one = D(())
    scratch = [
        V((rows, half), bf16), V((tiles, rows, TILE), f32), V((tiles, rows, TILE), f32),
        V((rows, hid), f32), V((rows, hid), f32), V((rows, hid), bf16), V((rows, emb), f32),
        V((nc, mine, emb), bf16), V((nc, mine, emb), bf16), V((mine, emb), f32),
        V((total, emb), bf16), V((mine, total), f32), V((mine, total), bf16),
        V((mine, emb), f32), V((rows, emb), bf16), V((tiles, nd * nr * rows, TILE), bf16),
        V((nd * nr * rows, width), bf16), V((nd, mine, width), bf16),
        V((3 + nc + nd, 2, total), f32),
        V((nd, hid, lanes), bf16), V((nd, hid, lanes), f32), V((nd, hid, lanes), bf16),
        V((nd, hid, lanes), bf16), V((nd, hid, lanes), bf16),
    ]
    sems = [
        one, D((tiles,)), D((nd,)), D((nc, nd)), D((nc,)), D((nc,)),
        one, D((nc,)), D((nd,)), D((nc,)), D((nc,)),
        D((nd,)), D((nd,)), D((nd,)), D((nc, 2 * nd)), D((nd + 1, tiles)), D((nd + 1, tiles)), D((2 * nd, tiles)),
        one, D((nd,)), D((nd,)),
    ]
    scratch += [s for s in sems for _ in range(2)]
    fig, capt, gwi, gwo = pl.pallas_call(
        functools.partial(kernel, nd, nr, nc),
        out_shape=(
            jax.ShapeDtypeStruct((rows, 128), f32),
            jax.ShapeDtypeStruct((1, total), f32),
            jax.ShapeDtypeStruct((width, hid), f32),
            jax.ShapeDtypeStruct((hid, lanes), f32),
        ),
        in_specs=[pl.BlockSpec(memory_space=V)] * 6,
        out_specs=[pl.BlockSpec(memory_space=V)] * 4,
        scratch_shapes=scratch,
        compiler_params=pltpu.CompilerParams(
            collective_id=0, has_side_effects=True, vmem_limit_bytes=60 * 2**20
        ),
    )(features, w_in, w_out, captions, pos, ids)
    slot = (r * nc + c) * nd + d
    cap_terms = lax.dynamic_slice_in_dim(capt[0], slot * cap, cap, 0)
    return fig[:, 0], cap_terms, gwi, gwo


def on_device(features, w_in, w_out, captions, positive):
    nd, nr, nc = (lax.axis_size(a) for a in ("dp", "row", "col"))
    groups = nd * nr
    small = groups * features.shape[0] <= 2048 and nr == 2 and nd > 1 and nc > 1
    even = (nd * captions.shape[0]) % 128 == 0 and features.shape[1] % (128 * groups) == 0 and w_out.shape[1] % (128 * groups) == 0
    body = joined if small and even else plain
    return body(features, w_in, w_out, captions, positive)


def solution(mesh):
    placed = (
        P(("dp", "row"), None),
        P("row", "col"),
        P("col", None),
        P(("dp", "row", "col"), None),
        P(("dp", "row")),
    )
    return jax.shard_map(
        on_device,
        mesh=mesh,
        in_specs=placed,
        out_specs=(
            P(("dp", "row")),
            P(("dp", "row", "col")),
            P(("dp", "row"), "col"),
            P("col", ("dp", "row")),
        ),
        check_vma=False,
    )
```
